32 devices in a mesh: gx: 8 (over z, x), gy: 4 (over y, core).
Axes of the slice: x: 2, y: 2, z: 4, core: 2. Of those that a mesh axis runs over, the one named last changes fastest.
Arguments:
- field: float32 [32, 64, 16, 384], P('gx', 'gy'), may hold values from -6 to 6
- inv_material: float32 [32, 64, 16], P('gx', 'gy'), may hold values from 0.5 to 2
- stiffness: bfloat16 [384, 384], replicated, may hold values from -0.15625 to 0.15625
- lift: bfloat16 [576, 384], replicated, may hold values from -1.25 to 1.25
- projection: bfloat16 [96, 64], replicated, may hold values from -0.625 to 0.625
- back_lift: bfloat16 [64, 384], replicated, may hold values from -0.75 to 0.75
- op_blocks: bfloat16 [8, 4, 64, 64], replicated, may hold values from -0.375 to 0.375
- op_columns: int32 [8, 4], replicated, may hold values from 0 to 7
- panel_dest: int32 [2048, 1], P(('gx', 'gy')), may hold values from 0 to 31; in each aligned block of 64 rows (0 to 63, 64 to 127, ...) at most 4 rows name the same one
- panel_anchor: int32 [2048], P(('gx', 'gy')), may hold values from 0 to 7
Outputs:
- advanced: float32 [32, 64, 16, 384], P('gx', 'gy')
The draws below stay inside these ranges and needn't reach their ends.
Inputs may be any that keep to these rules, and one draw needn't show every extreme that they name: `panel_dest`: among the 64 panels of one device no brick is named more than 4 times; some device names one brick exactly 4 times.
All inputs are finite; a program needn't handle non-finite values.
Results may differ from the reference program's by a relative error of at most 0.0084.
Values may be sent and summed in bfloat16 or wider, within the bound.
A program may use at most 128 MiB of HBM per device.

```python
import math
import jax
import jax.numpy as jnp
import numpy as np
from jax import lax

EX = 4
EY = 16
EZ = 16
NBLK = 8
KB = 4
NXE = 32
NYE = 64
PAN_DEV = 64
PANELS = 2048
CAP = 4
N_GX = 8
N_GY = 4
DEVICES = 32


def place_ends(array, stream_key, smallest, largest):
    place = [jax.random.randint(jax.random.fold_in(stream_key, axis), (), 0, length) for axis, length in enumerate(array.shape)]
    longest = array.shape.index(max(array.shape))
    next_to = place[:longest] + [(place[longest] + 1) % array.shape[longest]] + place[longest + 1:]
    return array.at[tuple(place)].set(smallest).at[tuple(next_to)].set(largest)


def levels(key, dims, shards, low, largest):
    def one(axis_at, blocks):
        steps = jax.random.uniform(jax.random.fold_in(jax.random.fold_in(key, 6), axis_at), (blocks,), jnp.float32, low / len(shards), largest / len(shards))
        return jnp.repeat(jnp.exp(steps), dims[axis_at] // blocks).reshape((-1,) + (1,) * (len(dims) - axis_at - 1))

    factor_of = one(*shards[0])
    for cut in shards[1:]:
        factor_of = factor_of * one(*cut)
    return factor_of


def routed_block(stream_key, own, number, rows, count, top, reach, slope):
    sequence = jax.random.permutation(stream_key, count)
    packed, common = load_shares(count, rows * top, reach, slope, True), load_shares(count, rows * top, reach, slope, False)
    places = jnp.arange(count)

    def named(sizes, rotation):
        used = int((sizes > 0).sum())
        fixed = max(1, used // 4)
        shifted = fixed + (places - fixed + rotation * (used - fixed)) % max(1, count - fixed)
        return jnp.zeros((count,), jnp.int32).at[sequence[jnp.where(places < fixed, places, shifted)]].set(jnp.asarray(sizes, jnp.int32))

    sizes = jnp.where(number % 4 == 0, named(packed, number // 4), named(common, number - number // 4 - 1))
    mixed = jax.random.permutation(jax.random.fold_in(own, 3), count)
    donor, taker = mixed[0:count // 2 * 2:2], mixed[1:count // 2 * 2:2]
    margin = jnp.minimum(sizes[donor] - 1, reach - sizes[taker]) // 2
    margin = jnp.where((donor == sequence[0]) | (taker == sequence[0]) | (sizes[taker] == 0), 0, jnp.maximum(margin, 0))
    shifted = jax.random.randint(jax.random.fold_in(own, 4), (count // 2,), 0, 1 << 20) % (margin + 1)
    sizes = sizes.at[donor].add(-shifted).at[taker].add(shifted)
    items = jnp.searchsorted(jnp.cumsum(sizes), jnp.arange(rows * top), side="right").astype(jnp.int32)
    listing = items.reshape(top, rows).T
    listing = listing[jax.random.permutation(jax.random.fold_in(own, 1), rows)]
    rotation = jax.random.randint(jax.random.fold_in(own, 2), (rows, 1), 0, top)
    return jnp.take_along_axis(listing, (jnp.arange(top)[None, :] + rotation) % top, axis=1)


def load_shares(amount, total, reach, slope, full):
    portions = [(1 << 20) // math.isqrt(grade ** slope) + 1 for grade in range(1, amount + 1)]
    largest = reach if full else min(reach, max(-(-total // amount), total * portions[0] // sum(portions)))
    least = 1 if total - largest >= amount - 1 else 0
    given, surplus = [largest] + [least] * (amount - 1), total - largest - least * (amount - 1)
    while surplus > 0:
        candidates = [i for i in range(1, amount) if given[i] < largest] or [i for i in range(1, amount) if given[i] < reach]
        mass, budget = sum([portions[i] for i in candidates]), surplus
        for i in candidates:
            more = min(reach - given[i], max(1, budget * portions[i] // mass), surplus)
            given[i] = given[i] + more
            surplus = surplus - more
    return np.array(given)


def centred(key, extent, deviation, reach, cuts=(), held_as=jnp.bfloat16):
    level = levels(key, extent, cuts, -0.22, 0.18) if cuts else 1.0
    drawn = jax.random.normal(key, extent, jnp.float32) * deviation * level
    return jnp.minimum(jnp.maximum(drawn, -reach), reach).astype(held_as)


def setup_inputs(seed: int = 0) -> dict:
    seeds = jax.random.split(jax.random.key(seed), 11)
    field = centred(seeds[0], (NXE, NYE, EZ, 384), 1.0, 6.0, ((0, 8), (1, 4)), jnp.float32)
    inv_material = jnp.clip(jnp.exp(math.log(2.0) - 1.3862944 * jax.random.uniform(seeds[1], (NXE, NYE, EZ), jnp.float32) ** levels(seeds[1], (NXE, NYE, EZ), ((0, 8), (1, 4)), -0.2, 0.2)), 0.5, 2.0)
    stiffness = centred(seeds[2], (384, 384), 1536 ** -0.5, 0.15625)
    lift = centred(seeds[3], (576, 384), 24 ** -0.5, 1.25)
    projection = centred(seeds[4], (96, 64), 96 ** -0.5, 0.625)
    back_lift = centred(seeds[5], (64, 384), 64 ** -0.5, 0.75)
    op_blocks = centred(seeds[6], (NBLK, KB, 64, 64), 256 ** -0.5, 0.375)
    op_columns = place_ends(jax.random.randint(seeds[7], (NBLK, KB), 0, NBLK), jax.random.fold_in(seeds[7], 1), 0, NBLK - 1).astype(jnp.int32)
    panel_dest_keys = jax.random.split(jax.random.fold_in(seeds[8], 1), PANELS // PAN_DEV)
    panel_dest_turns = jax.random.permutation(jax.random.fold_in(seeds[8], 3), PANELS // PAN_DEV)
    panel_dest = jax.vmap(lambda own, number: routed_block(jax.random.fold_in(seeds[8], 2), own, number, PAN_DEV, DEVICES, 1, CAP, 2))(panel_dest_keys, panel_dest_turns).reshape((PANELS, 1))
    panel_anchor = place_ends(jax.random.randint(seeds[9], (PANELS,), 0, NBLK), jax.random.fold_in(seeds[9], 1), 0, NBLK - 1).astype(jnp.int32)
    return dict(field=field, inv_material=inv_material, stiffness=stiffness, lift=lift, projection=projection, back_lift=back_lift, op_blocks=op_blocks, op_columns=op_columns, panel_dest=panel_dest, panel_anchor=panel_anchor)


step_size = 0.25


def face_traces(tr):
    lead = tr.shape[:3]
    shape = lead + (96,)
    return (tr[..., 0, :, :].reshape(shape), tr[..., 3, :, :].reshape(shape),
            tr[..., :, 0, :].reshape(shape), tr[..., :, 3, :].reshape(shape),
            tr[..., 0].reshape(shape), tr[..., 3].reshape(shape))


def lower_of(arr, axis):
    size = arr.shape[axis]
    zero = jnp.zeros_like(lax.slice_in_dim(arr, 0, 1, axis=axis))
    return jnp.concatenate([zero, lax.slice_in_dim(arr, 0, size - 1, axis=axis)], axis)


def upper_of(arr, axis):
    size = arr.shape[axis]
    zero = jnp.zeros_like(lax.slice_in_dim(arr, 0, 1, axis=axis))
    return jnp.concatenate([lax.slice_in_dim(arr, 1, size, axis=axis), zero], axis)


def rate(section, inv_material, stiffness, lift, projection, back_lift, op_blocks, op_columns, dest, anchor):
    nxe, nye, nze = section.shape[:3]
    devices = N_GX * N_GY
    sb = section.astype(jnp.bfloat16)
    tr = sb.reshape((nxe, nye, nze, 6, 4, 4, 4))
    xlo, xhi, ylo, yhi, zlo, zhi = face_traces(tr)
    f32 = jnp.float32
    jumps = jnp.concatenate([
        lower_of(xhi, 0).astype(f32) - xlo.astype(f32), upper_of(xlo, 0).astype(f32) - xhi.astype(f32),
        lower_of(yhi, 1).astype(f32) - ylo.astype(f32), upper_of(ylo, 1).astype(f32) - yhi.astype(f32),
        lower_of(zhi, 2).astype(f32) - zlo.astype(f32), upper_of(zlo, 2).astype(f32) - zhi.astype(f32)], -1).astype(jnp.bfloat16)
    volume = jnp.dot(sb.reshape(-1, 384), stiffness, preferred_element_type=f32)
    faces = jnp.dot(jumps.reshape(-1, 576), lift, preferred_element_type=f32)
    total = (volume + faces).reshape(nxe, nye, nze, 384)
    tops = zhi[:, :, nze - 1, :]
    tops = tops.reshape(N_GX, EX, N_GY, EY, 96).transpose(0, 2, 1, 3, 4).reshape(-1, 96)
    u = jnp.dot(tops, projection, preferred_element_type=f32).astype(jnp.bfloat16)
    ids = (dest * NBLK + anchor).astype(jnp.int32)
    grid = jax.ops.segment_sum(u.astype(f32), ids, num_segments=devices * NBLK)
    grid = grid.reshape(devices, NBLK, 64).astype(jnp.bfloat16)
    gsel = grid[:, op_columns]
    w = jnp.einsum('dikc,ikce->die', gsel.astype(f32), op_blocks.astype(f32)).astype(jnp.bfloat16)
    v = w.reshape(devices * NBLK, 64)[ids]
    bvals = jnp.dot(v, back_lift, preferred_element_type=f32)
    bvals = bvals.reshape(N_GX, N_GY, EX, EY, 384).transpose(0, 2, 1, 3, 4).reshape(nxe, nye, 384)
    total = total.at[:, :, nze - 1, :].add(bvals)
    return inv_material[..., None] * total


def reference(field, inv_material, stiffness, lift, projection, back_lift, op_blocks, op_columns, panel_dest, panel_anchor):
    dest = panel_dest[:, 0]

    def evaluate(section):
        return rate(section, inv_material, stiffness, lift, projection, back_lift, op_blocks, op_columns, dest, panel_anchor)

    k_one = evaluate(field)
    k_two = evaluate(field + (step_size / 2) * k_one)
    k_three = evaluate(field + (step_size / 2) * k_two)
    k_four = evaluate(field + step_size * k_three)
    return field + (step_size / 6) * (k_one + 2.0 * k_two + 2.0 * k_three + k_four)
```

```python
import functools

import jax
import jax.numpy as jnp
import numpy as np
from jax import lax
from jax.experimental import pallas as pl
from jax.experimental.pallas import tpu as pltpu
from jax.sharding import PartitionSpec as P

NBLK = 8
STEP = 0.25
F32 = jnp.float32
BF16 = jnp.bfloat16
MESH = pl.DeviceIdType.MESH


def selectors():
    nodes = np.arange(384).reshape(6, 4, 4, 4)
    faces = (
        nodes[:, 0], nodes[:, 3], nodes[:, :, 0], nodes[:, :, 3], nodes[..., 0], nodes[..., 3],
    )
    sel = np.zeros((384, 768), np.float32)
    for f, face in enumerate(faces):
        sel[face.reshape(-1), 128 * f + np.arange(96)] = 1
    return sel


def dot(a, b):
    return jnp.dot(a, b, preferred_element_type=F32)


def kernel(
    nx, ny, field, inv, stiff, lift, proj, back_lift, ops, col_code, send_code, recv_code, sel, out,
    tot, acc, sb, yz, xhi, xlo, yhi_send, ylo_send, x_low, x_high, y_low, y_high, lift_pad, top_w,
    back_w, op_w, place_send, place_recv, grid_mask, a_send, a_recv, b_send, b_recv, stack, top,
    a_ssem, a_rsem, b_ssem, b_rsem, h_ssem, h_rsem,
):
    n = nx * ny
    gx, gy = lax.axis_index("gx"), lax.axis_index("gy")
    ex_n, ez_n = 4, 16
    per = field.shape[0] // ex_n
    rows = per * ez_n

    def peer(i):
        return (lax.rem(gx + i // ny, nx), lax.rem(gy + lax.rem(i, ny), ny))

    barrier = pltpu.get_barrier_semaphore()

    @pl.loop(1, n)
    def _(i):
        pl.semaphore_signal(barrier, inc=1, device_id=peer(i), device_id_type=MESH)

    lift_pad[...] = jnp.zeros_like(lift_pad)
    for f in range(6):
        lift_pad[128 * f : 128 * f + 96, :] = lift[96 * f : 96 * f + 96, :]
    lane64 = lax.broadcasted_iota(jnp.int32, (64, 128), 1)
    row64 = lax.broadcasted_iota(jnp.int32, (64, 128), 0)
    to_left = (lane64 == row64).astype(F32).astype(BF16)
    to_right = (lane64 == row64 + 64).astype(F32).astype(BF16)
    source = dot(sel[:, 640:736], proj[...]).astype(BF16)
    top_w[:, 0:128] = dot(source, to_left).astype(BF16)
    top_w[:, 128:256] = dot(source, to_right).astype(BF16)
    back_w[...] = jnp.zeros_like(back_w)
    back_w[0:64, :] = back_lift[...]
    back_w[192:256, :] = back_lift[...]
    for q in range(NBLK // 2):
        for r in range(4):
            block = (
                dot(ops[2 * q, r], to_left) + dot(ops[2 * q + 1, r], to_right)
            ).astype(BF16)
            op_w[128 * r : 128 * r + 64, 128 * q : 128 * q + 128] = block
            op_w[128 * r + 64 : 128 * r + 128, 128 * q : 128 * q + 128] = block
    place_send[...] = jnp.where(
        lax.broadcasted_iota(jnp.int32, (4 * n, 128), 0) == send_code[...], 1.0, 0.0
    ).astype(BF16)
    place_recv[...] = jnp.where(
        lax.broadcasted_iota(jnp.int32, (128, 4 * n), 1) == recv_code[...], 1.0, 0.0
    ).astype(BF16)
    half = lax.broadcasted_iota(jnp.int32, (32, 128), 1) // 64
    for q in range(4):
        grid_mask[q] = jnp.where(col_code[...] == 2 * q + half, 1.0, 0.0)
    diagonal = jnp.where(
        lax.broadcasted_iota(jnp.int32, (NBLK, 512), 1) // 64
        == lax.broadcasted_iota(jnp.int32, (NBLK, 512), 0),
        1.0,
        0.0,
    )
    tot[...] = jnp.zeros_like(tot)
    acc[...] = jnp.zeros_like(acc)
    top[...] = field[:, ez_n - 1, :]

    @pl.when(gx == 0)
    def _():
        x_low[...] = jnp.zeros_like(x_low)

    @pl.when(gx == nx - 1)
    def _():
        x_high[...] = jnp.zeros_like(x_high)

    @pl.when(gy == 0)
    def _():
        y_low[...] = jnp.zeros_like(y_low)

    @pl.when(gy == ny - 1)
    def _():
        y_high[...] = jnp.zeros_like(y_high)

    pl.semaphore_wait(barrier, n - 1)

    z_at = lax.rem(lax.broadcasted_iota(jnp.int32, (rows, 128), 0), ez_n)
    not_first = jnp.where(z_at == 0, 0.0, 1.0)
    not_last = jnp.where(z_at == ez_n - 1, 0.0, 1.0)

    @pl.loop(0, 4)
    def _(s):
        c = jnp.where(s == 0, 0.0, jnp.where(s == 3, STEP, STEP / 2)).astype(F32)
        b = jnp.where(s == 0, 0.0, jnp.where(s == 1, 1.0, 2.0)).astype(F32)

        def halo(k, src, dst, dx, dy):
            return pltpu.make_async_remote_copy(
                src_ref=src, dst_ref=dst.at[s], send_sem=h_ssem.at[k], recv_sem=h_rsem.at[k, s],
                device_id=(gx + dx, gy + dy), device_id_type=MESH,
            )

        halos = (
            (halo(0, xhi.at[4], x_low, 1, 0), gx < nx - 1, gx > 0),
            (halo(1, xlo.at[0], x_high, -1, 0), gx > 0, gx < nx - 1),
            (halo(2, yhi_send, y_low, 0, 1), gy < ny - 1, gy > 0),
            (halo(3, ylo_send, y_high, 0, -1), gy > 0, gy < ny - 1),
        )

        pair = dot(top[...].astype(BF16), top_w[...])
        both = jnp.concatenate([pair[:, 0:128], pair[:, 128:256]], axis=0).astype(BF16)
        sums = dot(place_send[...], both)
        for j in range(n):
            a_send[j] = sums[4 * j : 4 * j + 4, :]

        def a_copy(i):
            return pltpu.make_async_remote_copy(
                src_ref=a_send.at[i], dst_ref=a_recv.at[s, i], send_sem=a_ssem,
                recv_sem=a_rsem.at[s], device_id=peer(i), device_id_type=MESH,
            )

        @pl.loop(1, n)
        def _(i):
            a_copy(i).start()

        @pl.loop(0, ex_n)
        def _(ex):
            at = pl.ds(ex * per, per)
            k = [
                tot[at, :, 128 * t : 128 * t + 128] * inv[at]
                for t in range(3)
            ]
            k = jnp.concatenate(k, axis=2)
            acc[at] = acc[at] + b * k
            sec = (field[at] + c * k).astype(BF16)
            sb[at] = sec
            flat = sec.reshape(rows, 384)
            x_both = dot(flat, sel[:, 0:256]).astype(BF16)
            xlo[ex] = x_both[:, 0:128]
            xhi[ex + 1] = x_both[:, 128:256]
            y_both = dot(flat, sel[:, 256:512]).astype(BF16)
            yz[ex, :, 0:256] = y_both
            ylo_send[ex] = y_both[0:16, 0:128]
            yhi_send[ex] = y_both[rows - 16 : rows, 128:256]
            yz[ex, :, 256:512] = dot(flat, sel[:, 512:768]).astype(BF16)

        for copy, sends, _r in halos:
            pl.when(sends)(copy.start)

        @pl.loop(0, ex_n)
        def _(ex):
            at = pl.ds(ex * per, per)
            zlo = yz[ex, :, 256:384].astype(F32)
            zhi = yz[ex, :, 384:512].astype(F32)
            below = pltpu.roll(zhi, 1, 0) * not_first
            above = pltpu.roll(zlo, rows - 1, 0) * not_last
            jump = jnp.concatenate(
                [(below - zlo).astype(BF16), (above - zhi).astype(BF16)], axis=1
            )
            got = dot(sb[at].reshape(rows, 384), stiff[...]) + dot(jump, lift_pad[512:768, :])
            tot[at] = got.reshape(per, ez_n, 384)

        a_all = a_recv.at[s, pl.ds(1, n - 1)]
        pltpu.make_async_copy(a_all, a_all, a_rsem.at[s]).wait()
        grid = a_send[0]
        for j in range(1, n):
            grid = grid + a_recv[s, j]
        grid = grid.astype(BF16).astype(F32)
        picked = grid_mask[0] * grid[0:1]
        for q in range(1, 4):
            picked = picked + grid_mask[q] * grid[q : q + 1]
        wide = jnp.concatenate([picked[8 * r : 8 * r + 8] for r in range(4)], axis=1)
        fields = jnp.sum(dot(wide.astype(BF16), op_w[...]) * diagonal, axis=0, keepdims=True)
        fields = fields.astype(BF16).astype(F32)
        for q in range(4):
            b_send[q : q + 1, :] = fields[:, 128 * q : 128 * q + 128]

        def b_copy(i):
            return pltpu.make_async_remote_copy(
                src_ref=b_send, dst_ref=b_recv.at[s, i], send_sem=b_ssem,
                recv_sem=b_rsem.at[s], device_id=peer(i), device_id_type=MESH,
            )

        @pl.loop(1, n)
        def _(i):
            b_copy(i).start()

        for copy, _s, receives in halos:
            pl.when(receives)(copy.wait_recv)
        for copy, sends, _r in halos:
            pl.when(sends)(copy.wait_send)
        xhi[0] = x_low[s]
        xlo[4] = x_high[s]

        @pl.loop(0, ex_n)
        def _(ex):
            at = pl.ds(ex * per, per)
            own_lo, own_hi = xlo[ex].astype(F32), xhi[ex + 1].astype(F32)
            jump_x = jnp.concatenate(
                [
                    (xhi[ex].astype(F32) - own_lo).astype(BF16),
                    (xlo[ex + 1].astype(F32) - own_hi).astype(BF16),
                ],
                axis=1,
            )
            ylo, yhi = yz[ex, :, 0:128].astype(F32), yz[ex, :, 128:256].astype(F32)
            low = jnp.concatenate([y_low[s, ex].astype(F32), yhi[0 : rows - 16]], axis=0)
            high = jnp.concatenate([ylo[16:rows], y_high[s, ex].astype(F32)], axis=0)
            jump_y = jnp.concatenate([(low - ylo).astype(BF16), (high - yhi).astype(BF16)], axis=1)
            got = dot(jump_x, lift_pad[0:256, :]) + dot(jump_y, lift_pad[256:512, :])
            tot[at] = tot[at] + got.reshape(per, ez_n, 384)

        b_all = b_recv.at[s, pl.ds(1, n - 1)]
        pltpu.make_async_copy(b_all, b_all, b_rsem.at[s]).wait()
        stack[0:4, :] = b_send[...]
        for j in range(1, n):
            stack[4 * j : 4 * j + 4, :] = b_recv[s, j]
        at_panels = dot(place_recv[...], stack[...].astype(BF16)).astype(BF16)
        at_panels = jnp.concatenate([at_panels[0:64], at_panels[64:128]], axis=1)
        top_tot = tot[:, ez_n - 1, :] + dot(at_panels, back_w[...])
        tot[:, ez_n - 1, :] = top_tot
        inv_top = inv[:, ez_n - 1, :]
        c_next = jnp.where(s == 2, STEP, STEP / 2).astype(F32)
        top[...] = field[:, ez_n - 1, :] + c_next * (
            jnp.concatenate([inv_top, inv_top, inv_top], axis=1) * top_tot
        )
        a_out = a_send.at[pl.ds(1, n - 1)]
        pltpu.make_async_copy(a_out, a_out, a_ssem).wait()
        pltpu.make_async_copy(b_all, b_all, b_ssem).wait()

    @pl.loop(0, ex_n)
    def _(ex):
        at = pl.ds(ex * per, per)
        for t in range(3):
            lanes = slice(128 * t, 128 * t + 128)
            out[at, :, lanes] = field[at, :, lanes] + (STEP / 6) * (
                acc[at, :, lanes] + tot[at, :, lanes] * inv[at]
            )


def body(
    nx, ny, field, inv_material, stiffness, lift, projection, back_lift, op_blocks, op_columns,
    panel_dest, panel_anchor,
):
    ex_n, ey_n, ez_n = field.shape[:3]
    panels, n = ex_n * ey_n, nx * ny
    rows = ey_n * ez_n
    gx, gy = lax.axis_index("gx"), lax.axis_index("gy")
    dest = panel_dest[:, 0]
    dx, dy = dest // ny, dest % ny
    pair, odd = panel_anchor // 2, panel_anchor % 2
    ahead = ((dx - gx + nx) % nx * ny + (dy - gy + ny) % ny) * 4 + pair
    behind = ((gx - dx + nx) % nx * ny + (gy - dy + ny) % ny) * 4 + pair
    send_code = jnp.stack([jnp.where(odd == p, ahead, -1) for p in (0, 1)]).reshape(1, 128)
    recv_code = jnp.stack([jnp.where(odd == p, behind, -1) for p in (0, 1)]).reshape(128, 1)
    col_code = op_columns.T.reshape(32, 1)
    inv = jnp.broadcast_to(inv_material[..., None], (ex_n, ey_n, ez_n, 128))
    vmem = pl.BlockSpec(memory_space=pltpu.VMEM)
    out = pl.pallas_call(
        functools.partial(kernel, nx, ny),
        out_shape=jax.ShapeDtypeStruct((panels, ez_n, 384), F32),
        in_specs=[vmem] * 11,
        out_specs=vmem,
        scratch_shapes=[
            pltpu.VMEM((panels, ez_n, 384), F32),
            pltpu.VMEM((panels, ez_n, 384), F32),
            pltpu.VMEM((panels, ez_n, 384), BF16),
            pltpu.VMEM((ex_n, rows, 512), BF16),
            pltpu.VMEM((ex_n + 1, rows, 128), BF16),
            pltpu.VMEM((ex_n + 1, rows, 128), BF16),
            pltpu.VMEM((ex_n, 16, 128), BF16),
            pltpu.VMEM((ex_n, 16, 128), BF16),
            pltpu.VMEM((4, rows, 128), BF16),
            pltpu.VMEM((4, rows, 128), BF16),
            pltpu.VMEM((4, ex_n, 16, 128), BF16),
            pltpu.VMEM((4, ex_n, 16, 128), BF16),
            pltpu.VMEM((768, 384), BF16),
            pltpu.VMEM((384, 256), BF16),
            pltpu.VMEM((256, 384), BF16),
            pltpu.VMEM((512, 512), BF16),
            pltpu.VMEM((4 * n, 128), BF16),
            pltpu.VMEM((128, 4 * n), BF16),
            pltpu.VMEM((4, 32, 128), F32),
            pltpu.VMEM((n, 4, 128), F32),
            pltpu.VMEM((4, n, 4, 128), F32),
            pltpu.VMEM((4, 128), F32),
            pltpu.VMEM((4, n, 4, 128), F32),
            pltpu.VMEM((4 * n, 128), F32),
            pltpu.VMEM((panels, 384), F32),
            pltpu.SemaphoreType.DMA,
            pltpu.SemaphoreType.DMA((4,)),
            pltpu.SemaphoreType.DMA,
            pltpu.SemaphoreType.DMA((4,)),
            pltpu.SemaphoreType.DMA((4,)),
            pltpu.SemaphoreType.DMA((4, 4)),
        ],
        compiler_params=pltpu.CompilerParams(
            collective_id=0, has_side_effects=True, vmem_limit_bytes=48 * 2**20
        ),
    )(
        field.reshape(panels, ez_n, 384), inv.reshape(panels, ez_n, 128), stiffness, lift,
        projection, back_lift, op_blocks, col_code, send_code, recv_code,
        jnp.asarray(selectors(), BF16),
    )
    return out.reshape(ex_n, ey_n, ez_n, 384)


def solution(mesh):
    return jax.shard_map(
        functools.partial(body, mesh.shape["gx"], mesh.shape["gy"]),
        mesh=mesh,
        in_specs=(
            P("gx", "gy", None, None),
            P("gx", "gy", None),
            P(),
            P(),
            P(),
            P(),
            P(),
            P(),
            P(("gx", "gy"), None),
            P(("gx", "gy")),
        ),
        out_specs=P("gx", "gy", None, None),
        check_vma=False,
    )
```

```python
import functools

import jax
import jax.numpy as jnp
import numpy as np
from jax import lax
from jax.experimental import pallas as pl
from jax.experimental.pallas import tpu as pltpu
from jax.sharding import PartitionSpec as P

NBLK = 8
STEP = 0.25
F32 = jnp.float32
BF16 = jnp.bfloat16
MESH = pl.DeviceIdType.MESH


def selectors():
    nodes = np.arange(384).reshape(6, 4, 4, 4)
    faces = (
        nodes[:, 0], nodes[:, 3], nodes[:, :, 0], nodes[:, :, 3], nodes[..., 0], nodes[..., 3],
    )
    sel = np.zeros((384, 768), np.float32)
    for f, face in enumerate(faces):
        sel[face.reshape(-1), 128 * f + np.arange(96)] = 1
    return sel


def dot(a, b):
    return jnp.dot(a, b, preferred_element_type=F32)


def kernel(
    nx, ny, field_in, inv_in, stiff_in, lift_in, proj_in, back_in, ops_in, columns_in, dest_in,
    anchor_in, sel_in, out, field, inv_raw, stiff, lift, proj, back_lift, ops, columns, dest, anchor,
    sel, load_sem, inv, tot, acc, yz, xhi, xlo, yhi_send, ylo_send, x_low, x_high, y_low, y_high, lift_pad, top_w,
    back_w, op_w, place_send, place_recv, grid_mask, a_send, a_recv, b_send, b_recv, stack,
    first_send, first_recv, grid_sum, weight, reflect,
    a_ssem, a_rsem, b_ssem, b_rsem, h_ssem, h_rsem,
):
    n = nx * ny
    gx, gy = lax.axis_index("gx"), lax.axis_index("gy")
    ex_n, ez_n = 4, 16
    per = field.shape[0] // ex_n
    loads = [
        pltpu.make_async_copy(src, dst, load_sem.at[i])
        for i, (src, dst) in enumerate(
            (
                (columns_in, columns), (dest_in, dest), (anchor_in, anchor), (proj_in, proj),
                (sel_in, sel), (ops_in, ops), (back_in, back_lift), (lift_in, lift),
                (inv_in, inv_raw), (field_in, field), (stiff_in, stiff),
            )
        )
    ]
    for load in loads:
        load.start()
    rows = per * ez_n

    def peer(i):
        return (lax.rem(gx + i // ny, nx), lax.rem(gy + lax.rem(i, ny), ny))

    barrier = pltpu.get_barrier_semaphore()

    @pl.loop(1, n)
    def _(i):
        pl.semaphore_signal(barrier, inc=1, device_id=peer(i), device_id_type=MESH)

    for load in loads:
        load.wait()

    inv[...] = jnp.broadcast_to(inv_raw[...][:, :, None], inv.shape)
    lift_pad[...] = jnp.zeros_like(lift_pad)
    for f in range(6):
        lift_pad[128 * f : 128 * f + 96, :] = lift[96 * f : 96 * f + 96, :]
    lane64 = lax.broadcasted_iota(jnp.int32, (64, 128), 1)
    row64 = lax.broadcasted_iota(jnp.int32, (64, 128), 0)
    to_left = (lane64 == row64).astype(F32).astype(BF16)
    to_right = (lane64 == row64 + 64).astype(F32).astype(BF16)
    source = lax.dot_general(
        sel[:, 640:736], proj[...], (((1,), (1,)), ((), ())), preferred_element_type=F32
    ).astype(BF16)
    top_w[:, 0:128] = dot(source, to_left).astype(BF16)
    top_w[:, 128:256] = dot(source, to_right).astype(BF16)
    back_w[...] = jnp.zeros_like(back_w)
    back_w[0:64, :] = back_lift[...]
    back_w[192:256, :] = back_lift[...]
    for q in range(NBLK // 2):
        block = dot(ops[2 * q].reshape(256, 64), to_left) + dot(
            ops[2 * q + 1].reshape(256, 64), to_right
        )
        block = block.astype(BF16)
        lanes = slice(128 * q, 128 * q + 128)
        for r in range(4):
            piece = block[64 * r : 64 * r + 64]
            op_w[128 * r : 128 * r + 64, lanes] = piece
            op_w[128 * r + 64 : 128 * r + 128, lanes] = piece

    def codes(where, block, axis):
        dx, dy = where // ny, lax.rem(where, ny)
        pair, odd = block // 2, lax.rem(block, 2)
        if axis == 1:
            there = lax.rem(dx - gx + nx, nx) * ny + lax.rem(dy - gy + ny, ny)
        else:
            there = lax.rem(gx - dx + nx, nx) * ny + lax.rem(gy - dy + ny, ny)
        code = there * 4 + pair
        return jnp.concatenate([jnp.where(odd == p, code, -1) for p in (0, 1)], axis=axis)

    def column(row):
        size = row.shape[1]
        eye = lax.broadcasted_iota(jnp.int32, (size, size), 0) == lax.broadcasted_iota(
            jnp.int32, (size, size), 1
        )
        picked = jnp.where(eye, row.astype(F32), 0.0)
        return jnp.sum(picked, axis=1, keepdims=True).astype(jnp.int32)

    send_code = codes(dest[...], anchor[...], 1)
    recv_code = codes(column(dest[...]), column(anchor[...]), 0)
    place_send[...] = jnp.where(
        lax.broadcasted_iota(jnp.int32, (4 * n, 128), 0) == send_code, 1.0, 0.0
    ).astype(BF16)
    place_recv[...] = jnp.where(
        lax.broadcasted_iota(jnp.int32, (128, 4 * n), 1) == recv_code, 1.0, 0.0
    ).astype(BF16)
    half = lax.broadcasted_iota(jnp.int32, (8, 128), 1) // 64
    for r in range(4):
        named = column(columns[r : r + 1, :])
        for q in range(4):
            grid_mask[q, 8 * r : 8 * r + 8] = jnp.where(named == 2 * q + half, 1.0, 0.0)
    diagonal = jnp.where(
        lax.broadcasted_iota(jnp.int32, (NBLK, 512), 1) // 64
        == lax.broadcasted_iota(jnp.int32, (NBLK, 512), 0),
        1.0,
        0.0,
    )
    echo = dot(back_lift[...], top_w[:, 0:128]).astype(BF16)
    reflect[...] = jnp.zeros_like(reflect)
    reflect[0:64, :] = echo
    reflect[64:128, :] = dot(back_lift[...], top_w[:, 128:256]).astype(BF16)
    b_send[...] = jnp.zeros_like(b_send)
    tot[...] = jnp.zeros_like(tot)
    acc[...] = jnp.zeros_like(acc)
    inv_top = inv[:, ez_n - 1, :]
    left = lax.broadcasted_iota(jnp.int32, inv_top.shape, 1) < 64
    shares = jnp.concatenate(
        [jnp.where(left, inv_top, 0.0), jnp.where(left, 0.0, inv_top)], axis=0
    )
    coarse = shares.astype(BF16)
    fine = (shares - coarse.astype(F32)).astype(BF16)
    weights = dot(place_send[...], coarse) + dot(place_send[...], fine)

    def panel_sums(section):
        pair = dot(section.astype(BF16), top_w[...])
        both = jnp.concatenate([pair[:, 0:128], pair[:, 128:256]], axis=0).astype(BF16)
        return dot(place_send[...], both)

    sums = panel_sums(field[:, ez_n - 1, :])
    for j in range(n):
        first_send[j, 0:4] = sums[4 * j : 4 * j + 4, :]
        first_send[j, 4:8] = weights[4 * j : 4 * j + 4, :]

    @pl.when(gx == 0)
    def _():
        x_low[...] = jnp.zeros_like(x_low)

    @pl.when(gx == nx - 1)
    def _():
        x_high[...] = jnp.zeros_like(x_high)

    @pl.when(gy == 0)
    def _():
        y_low[...] = jnp.zeros_like(y_low)

    @pl.when(gy == ny - 1)
    def _():
        y_high[...] = jnp.zeros_like(y_high)

    pl.semaphore_wait(barrier, n - 1)

    def first_copy(i):
        return pltpu.make_async_remote_copy(
            src_ref=first_send.at[i], dst_ref=first_recv.at[i], send_sem=a_ssem,
            recv_sem=a_rsem.at[0], device_id=peer(i), device_id_type=MESH,
        )

    @pl.loop(1, n)
    def _(i):
        first_copy(i).start()

    z_at = lax.rem(lax.broadcasted_iota(jnp.int32, (rows, 128), 0), ez_n)
    not_first = jnp.where(z_at == 0, 0.0, 1.0)
    not_last = jnp.where(z_at == ez_n - 1, 0.0, 1.0)

    @pl.loop(0, 4)
    def _(s):
        c = jnp.where(s == 0, 0.0, jnp.where(s == 3, STEP, STEP / 2)).astype(F32)
        b = jnp.where(s == 0, 0.0, jnp.where(s == 1, 1.0, 2.0)).astype(F32)

        def halo(k, src, dst, dx, dy):
            return pltpu.make_async_remote_copy(
                src_ref=src, dst_ref=dst.at[s], send_sem=h_ssem.at[k], recv_sem=h_rsem.at[k, s],
                device_id=(gx + dx, gy + dy), device_id_type=MESH,
            )

        halos = (
            (halo(0, xhi.at[4], x_low, 1, 0), gx < nx - 1, gx > 0),
            (halo(1, xlo.at[0], x_high, -1, 0), gx > 0, gx < nx - 1),
            (halo(2, yhi_send, y_low, 0, 1), gy < ny - 1, gy > 0),
            (halo(3, ylo_send, y_high, 0, -1), gy > 0, gy < ny - 1),
        )

        @pl.loop(0, ex_n)
        def _(turn):
            ex = lax.rem(turn + ex_n - 1, ex_n)
            at = pl.ds(ex * per, per)
            k = [
                tot[at, :, 128 * t : 128 * t + 128] * inv[at]
                for t in range(3)
            ]
            k = jnp.concatenate(k, axis=2)
            acc[at] = acc[at] + b * k
            sec = (field[at] + c * k).astype(BF16)
            flat = sec.reshape(rows, 384)
            x_both = dot(flat, sel[:, 0:256]).astype(BF16)
            xlo[ex] = x_both[:, 0:128]
            xhi[ex + 1] = x_both[:, 128:256]
            y_both = dot(flat, sel[:, 256:512]).astype(BF16)
            yz[ex] = y_both
            ylo_send[ex] = y_both[0:16, 0:128]
            yhi_send[ex] = y_both[rows - 16 : rows, 128:256]
            for at_turn in range(2):
                copy, sends, _r = halos[at_turn]
                pl.when(jnp.logical_and(sends, turn == at_turn))(copy.start)
            z_both = dot(flat, sel[:, 512:768])
            zlo = z_both[:, 0:128]
            zhi = z_both[:, 128:256]
            below = pltpu.roll(zhi, 1, 0) * not_first
            above = pltpu.roll(zlo, rows - 1, 0) * not_last
            jump = jnp.concatenate(
                [(below - zlo).astype(BF16), (above - zhi).astype(BF16)], axis=1
            )
            got = dot(flat, stiff[...]) + dot(jump, lift_pad[512:768, :])
            tot[at] = got.reshape(per, ez_n, 384)

        for copy, sends, _r in halos[2:]:
            pl.when(sends)(copy.start)

        a_out = a_send.at[pl.ds(1, n - 1)]

        @pl.when(s == 0)
        def _():
            came = first_recv.at[pl.ds(1, n - 1)]
            pltpu.make_async_copy(came, came, a_rsem.at[0]).wait()
            pltpu.make_async_copy(came, came, a_ssem).wait()
            total = first_send[0]
            for j in range(1, n):
                total = total + first_recv[j]
            grid_sum[...] = total[0:4]
            weight[...] = total[4:8]

        @pl.when(s > 0)
        def _():
            a_all = a_recv.at[s, pl.ds(1, n - 1)]
            pltpu.make_async_copy(a_all, a_all, a_rsem.at[s]).wait()
            pltpu.make_async_copy(a_out, a_out, a_ssem).wait()
            total = a_send[0]
            for j in range(1, n):
                total = total + a_recv[s, j]
            fed = b_send[...].astype(BF16)
            back = jnp.concatenate(
                [
                    dot(fed[:, 0:64], reflect[0:64, :])[:, 0:64],
                    dot(fed[:, 64:128], reflect[64:128, :])[:, 64:128],
                ],
                axis=1,
            )
            grid_sum[...] = total + c * weight[...] * back

        grid = grid_sum[...].astype(BF16).astype(F32)
        picked = grid_mask[0] * grid[0:1]
        for q in range(1, 4):
            picked = picked + grid_mask[q] * grid[q : q + 1]
        wide = jnp.concatenate([picked[8 * r : 8 * r + 8] for r in range(4)], axis=1)
        fields = jnp.sum(dot(wide.astype(BF16), op_w[...]) * diagonal, axis=0, keepdims=True)
        fields = fields.astype(BF16).astype(F32)
        for q in range(4):
            b_send[q : q + 1, :] = fields[:, 128 * q : 128 * q + 128]

        def b_copy(i):
            return pltpu.make_async_remote_copy(
                src_ref=b_send, dst_ref=b_recv.at[s, i], send_sem=b_ssem,
                recv_sem=b_rsem.at[s], device_id=peer(i), device_id_type=MESH,
            )

        @pl.loop(1, n)
        def _(i):
            b_copy(i).start()

        for copy, _s, receives in halos:
            pl.when(receives)(copy.wait_recv)
        for copy, sends, _r in halos:
            pl.when(sends)(copy.wait_send)
        xhi[0] = x_low[s]
        xlo[4] = x_high[s]

        @pl.loop(0, ex_n)
        def _(ex):
            at = pl.ds(ex * per, per)
            own_lo, own_hi = xlo[ex].astype(F32), xhi[ex + 1].astype(F32)
            jump_x = jnp.concatenate(
                [
                    (xhi[ex].astype(F32) - own_lo).astype(BF16),
                    (xlo[ex + 1].astype(F32) - own_hi).astype(BF16),
                ],
                axis=1,
            )
            ylo, yhi = yz[ex, :, 0:128].astype(F32), yz[ex, :, 128:256].astype(F32)
            low = jnp.concatenate([y_low[s, ex].astype(F32), yhi[0 : rows - 16]], axis=0)
            high = jnp.concatenate([ylo[16:rows], y_high[s, ex].astype(F32)], axis=0)
            jump_y = jnp.concatenate([(low - ylo).astype(BF16), (high - yhi).astype(BF16)], axis=1)
            got = dot(jump_x, lift_pad[0:256, :]) + dot(jump_y, lift_pad[256:512, :])
            tot[at] = tot[at] + got.reshape(per, ez_n, 384)

        c_next = jnp.where(s == 2, STEP, STEP / 2).astype(F32)

        def a_copy(i):
            return pltpu.make_async_remote_copy(
                src_ref=a_send.at[i], dst_ref=a_recv.at[s + 1, i], send_sem=a_ssem,
                recv_sem=a_rsem.at[s + 1], device_id=peer(i), device_id_type=MESH,
            )

        @pl.when(s < 3)
        def _():
            inv_top = inv[:, ez_n - 1, :]
            inv_top = jnp.concatenate([inv_top, inv_top, inv_top], axis=1)
            sums = panel_sums(field[:, ez_n - 1, :] + c_next * (inv_top * tot[:, ez_n - 1, :]))
            for j in range(n):
                a_send[j] = sums[4 * j : 4 * j + 4, :]

            @pl.loop(1, n)
            def _(i):
                a_copy(i).start()

        b_all = b_recv.at[s, pl.ds(1, n - 1)]
        pltpu.make_async_copy(b_all, b_all, b_rsem.at[s]).wait()
        stack[0:4, :] = b_send[...]
        for j in range(1, n):
            stack[4 * j : 4 * j + 4, :] = b_recv[s, j]
        at_panels = dot(place_recv[...], stack[...].astype(BF16)).astype(BF16)
        at_panels = jnp.concatenate([at_panels[0:64], at_panels[64:128]], axis=1)
        tot[:, ez_n - 1, :] = tot[:, ez_n - 1, :] + dot(at_panels, back_w[...])
        pltpu.make_async_copy(b_all, b_all, b_ssem).wait()

    @pl.loop(0, ex_n)
    def _(ex):
        at = pl.ds(ex * per, per)
        for t in range(3):
            lanes = slice(128 * t, 128 * t + 128)
            out[at, :, lanes] = field[at, :, lanes] + (STEP / 6) * (
                acc[at, :, lanes] + tot[at, :, lanes] * inv[at]
            )


def body(
    nx, ny, field, inv_material, stiffness, lift, projection, back_lift, op_blocks, op_columns,
    panel_dest, panel_anchor,
):
    ex_n, ey_n, ez_n = field.shape[:3]
    panels, n = ex_n * ey_n, nx * ny
    rows = ey_n * ez_n
    hbm = pl.BlockSpec(memory_space=pltpu.HBM)
    vmem = pl.BlockSpec(memory_space=pltpu.VMEM)
    out = pl.pallas_call(
        functools.partial(kernel, nx, ny),
        out_shape=jax.ShapeDtypeStruct((panels, ez_n, 384), F32),
        in_specs=[hbm] * 11,
        out_specs=vmem,
        scratch_shapes=[
            pltpu.VMEM((panels, ez_n, 384), F32),
            pltpu.VMEM((panels, ez_n), F32),
            pltpu.VMEM(stiffness.shape, BF16),
            pltpu.VMEM(lift.shape, BF16),
            pltpu.VMEM(projection.shape[::-1], BF16),
            pltpu.VMEM(back_lift.shape, BF16),
            pltpu.VMEM(op_blocks.shape, BF16),
            pltpu.VMEM(op_columns.shape[::-1], jnp.int32),
            pltpu.VMEM((1, panels), jnp.int32),
            pltpu.VMEM((1, panels), jnp.int32),
            pltpu.VMEM((384, 768), BF16),
            pltpu.SemaphoreType.DMA((11,)),
            pltpu.VMEM((panels, ez_n, 128), F32),
            pltpu.VMEM((panels, ez_n, 384), F32),
            pltpu.VMEM((panels, ez_n, 384), F32),
            pltpu.VMEM((ex_n, rows, 256), BF16),
            pltpu.VMEM((ex_n + 1, rows, 128), BF16),
            pltpu.VMEM((ex_n + 1, rows, 128), BF16),
            pltpu.VMEM((ex_n, 16, 128), BF16),
            pltpu.VMEM((ex_n, 16, 128), BF16),
            pltpu.VMEM((4, rows, 128), BF16),
            pltpu.VMEM((4, rows, 128), BF16),
            pltpu.VMEM((4, ex_n, 16, 128), BF16),
            pltpu.VMEM((4, ex_n, 16, 128), BF16),
            pltpu.VMEM((768, 384), BF16),
            pltpu.VMEM((384, 256), BF16),
            pltpu.VMEM((256, 384), BF16),
            pltpu.VMEM((512, 512), BF16),
            pltpu.VMEM((4 * n, 128), BF16),
            pltpu.VMEM((128, 4 * n), BF16),
            pltpu.VMEM((4, 32, 128), F32),
            pltpu.VMEM((n, 4, 128), F32),
            pltpu.VMEM((4, n, 4, 128), F32),
            pltpu.VMEM((4, 128), F32),
            pltpu.VMEM((4, n, 4, 128), F32),
            pltpu.VMEM((4 * n, 128), F32),
            pltpu.VMEM((n, 8, 128), F32),
            pltpu.VMEM((n, 8, 128), F32),
            pltpu.VMEM((4, 128), F32),
            pltpu.VMEM((4, 128), F32),
            pltpu.VMEM((128, 128), BF16),
            pltpu.SemaphoreType.DMA,
            pltpu.SemaphoreType.DMA((4,)),
            pltpu.SemaphoreType.DMA,
            pltpu.SemaphoreType.DMA((4,)),
            pltpu.SemaphoreType.DMA((4,)),
            pltpu.SemaphoreType.DMA((4, 4)),
        ],
        compiler_params=pltpu.CompilerParams(
            collective_id=0, has_side_effects=True, vmem_limit_bytes=60 * 2**20
        ),
    )(
        field.reshape(panels, ez_n, 384), inv_material.reshape(panels, ez_n), stiffness, lift,
        projection.T, back_lift, op_blocks, op_columns.T, panel_dest.reshape(1, panels),
        panel_anchor.reshape(1, panels),
        jnp.asarray(selectors(), BF16),
    )
    return out.reshape(ex_n, ey_n, ez_n, 384)


def solution(mesh):
    return jax.shard_map(
        functools.partial(body, mesh.shape["gx"], mesh.shape["gy"]),
        mesh=mesh,
        in_specs=(
            P("gx", "gy", None, None),
            P("gx", "gy", None),
            P(),
            P(),
            P(),
            P(),
            P(),
            P(),
            P(("gx", "gy"), None),
            P(("gx", "gy")),
        ),
        out_specs=P("gx", "gy", None, None),
        check_vma=False,
    )
```
